1024 devices in a mesh: blk: 32 (over x, z_lo), group: 32 (over y, z_hi, core).
Axes of the slice: x: 4, y: 8, z: 16 (z_hi: 2, z_lo: 8; z = z_hi * 8 + z_lo), core: 2. Of those that a mesh axis runs over, the one named last changes fastest.
Arguments:
- images: bfloat16 [163840, 1152], P(('blk', 'group')), may hold values from -4 to 4
- texts: bfloat16 [163840, 1152], P(('blk', 'group')), may hold values from -4 to 4
- exponent_of_multiplier: float32 [1], replicated, may hold values from 1 to 2
- bias: float32 [1], replicated, may hold values from -3 to -1
Outputs:
- grad_images: float32 [163840, 1152], P(('blk', 'group'))
- grad_texts: float32 [163840, 1152], P(('blk', 'group'))
- loss_mean: float32 [1], replicated
- temp_grad: float32 [1], replicated
- bias_grad: float32 [1], replicated
The draws below stay inside these ranges and needn't reach their ends.
All inputs are finite; a program needn't handle non-finite values.
Results may differ from the reference program's by a relative error of at most 0.00055.
Values may be sent and summed in bfloat16 or wider, within the bound.
A program may use at most 32 MiB of HBM per device.

```python
import math
import jax
import jax.numpy as jnp
from jax import lax

D = 1152
ROWS_DEV = 160
SHIFTS = 4
ROWS = 163840
N_BLK = 32
N_GROUP = 32


def shared_direction(key):
    return jax.random.truncated_normal(jax.random.fold_in(key, 7), -4.0, 4.0, (D,), jnp.float32) / math.sqrt(D)


def build_rows(key, direction, noise_rows, strength, scale_lo, scale_hi):
    position = jnp.arange(ROWS, dtype=jnp.float32) / ROWS
    weight_rows = strength * position
    scales = jnp.exp(jax.random.uniform(key, (ROWS, 1), jnp.float32, math.log(scale_lo), math.log(scale_hi)))
    rows = scales * (noise_rows / math.sqrt(D) + weight_rows[:, None] * direction[None, :])
    return jnp.clip(rows, -4.0, 4.0).astype(jnp.bfloat16)


def draw_images(key, part):
    direction = shared_direction(key)
    key = jax.random.fold_in(key, 11)
    noise_key, scale_key = jax.random.split(key)
    noise_rows = jax.random.truncated_normal(noise_key, -4.0, 4.0, (ROWS, D), jnp.float32)
    return build_rows(scale_key, direction, noise_rows, 0.6, 2.0, 20.0)


def draw_texts(key, part):
    direction = shared_direction(key)
    key = jax.random.fold_in(key, 23)
    noise_key, scale_key = jax.random.split(key)
    noise_rows = jax.random.truncated_normal(noise_key, -4.0, 4.0, (ROWS, D), jnp.float32)
    return build_rows(scale_key, direction, noise_rows, 0.6, 2.0, 20.0)


def setup_inputs(seed: int = 0) -> dict:
    key_list = jax.random.split(jax.random.key(seed), 5)
    images = draw_images(jax.random.fold_in(key_list[4], 71), 0)
    texts = draw_texts(jax.random.fold_in(key_list[4], 71), 0)
    exponent_of_multiplier = jnp.clip(jax.random.uniform(key_list[2], (1,), jnp.float32, 1.0, 2.0), 1.0, 2.0)
    bias = jnp.clip(jax.random.uniform(key_list[3], (1,), jnp.float32, -3.0, -1.0), -3.0, -1.0)
    return {"images": images, "texts": texts, "exponent_of_multiplier": exponent_of_multiplier, "bias": bias}


norm_eps = 1e-06

def prepare(rows):
    widened = rows.astype(jnp.float32)
    length = jnp.sqrt(lax.optimization_barrier(jnp.sum(widened * widened, axis=-1, keepdims=True)) + norm_eps)
    unit_rows = widened / length
    return (unit_rows, length, unit_rows.astype(jnp.bfloat16))

def unnormalize(unit_rows, length, gradient):
    along = lax.optimization_barrier(jnp.sum(unit_rows * gradient, axis=-1, keepdims=True))
    return (gradient - unit_rows * along) / length

def crosswise_tile(picture_entry_segment, caption_entry_segment, inverse_sharpness, displaced_intercept, matching_indicator):
    angular_agreement = jnp.einsum('bgrd,bgqd->bgrq', picture_entry_segment, caption_entry_segment, precision=lax.Precision.HIGHEST)
    matching_scores = inverse_sharpness * angular_agreement + displaced_intercept
    if matching_indicator:
        label_sign = 2.0 * jnp.eye(angular_agreement.shape[-1], dtype=jnp.float32) - 1.0
    else:
        label_sign = -jnp.ones((angular_agreement.shape[-1], angular_agreement.shape[-1]), jnp.float32)
    flipped = -label_sign * matching_scores
    objective_aggregate = jnp.sum(jax.nn.softplus(flipped))
    logistic_derivatives = -label_sign * jax.nn.sigmoid(flipped)
    target_sign_factors = (inverse_sharpness * logistic_derivatives).astype(jnp.bfloat16).astype(jnp.float32)
    picture_derivative_share = jnp.einsum('bgrq,bgqd->bgrd', target_sign_factors, caption_entry_segment, precision=lax.Precision.HIGHEST)
    caption_derivative_share = jnp.einsum('bgrq,bgrd->bgqd', target_sign_factors, picture_entry_segment, precision=lax.Precision.HIGHEST)
    accumulated_sums = jnp.stack([objective_aggregate, jnp.sum(logistic_derivatives * inverse_sharpness * angular_agreement), jnp.sum(logistic_derivatives)])
    return (picture_derivative_share, caption_derivative_share, accumulated_sums)

def flip_groups(blocks):
    half = N_GROUP // 2
    return blocks.reshape(N_BLK, 2, half, ROWS_DEV, D)[:, ::-1].reshape(N_BLK, N_GROUP, ROWS_DEV, D)

def reference(images, texts, exponent_of_multiplier, bias):
    img_unit, img_len, picture_reduced_accuracy = prepare(images)
    txt_unit, txt_len, txt_bf = prepare(texts)
    block_shape = (N_BLK, N_GROUP, ROWS_DEV, D)
    picture_segment_sequence = picture_reduced_accuracy.astype(jnp.float32).reshape(block_shape)
    txt_blocks = txt_bf.astype(jnp.float32).reshape(block_shape)
    inverse_sharpness = jnp.exp(exponent_of_multiplier[0])
    displaced_intercept = bias[0]
    grad_img = jnp.zeros(block_shape, jnp.float32)
    grad_txt = jnp.zeros(block_shape, jnp.float32)
    accumulated_sums = jnp.zeros((3,), jnp.float32)
    for segment_displacement in range(SHIFTS):
        previously_matched = jnp.roll(txt_blocks, segment_displacement, axis=0)
        picture_derivative_share, caption_derivative_share, interim_objective = crosswise_tile(picture_segment_sequence, previously_matched, inverse_sharpness, displaced_intercept, segment_displacement == 0)
        grad_img = grad_img + picture_derivative_share
        grad_txt = grad_txt + jnp.roll(caption_derivative_share, -segment_displacement, axis=0)
        accumulated_sums = accumulated_sums + interim_objective
    previously_matched = flip_groups(jnp.roll(txt_blocks, SHIFTS - 1, axis=0))
    picture_derivative_share, caption_derivative_share, interim_objective = crosswise_tile(picture_segment_sequence, previously_matched, inverse_sharpness, displaced_intercept, False)
    grad_img = grad_img + picture_derivative_share
    grad_txt = grad_txt + jnp.roll(flip_groups(caption_derivative_share), -(SHIFTS - 1), axis=0)
    accumulated_sums = accumulated_sums + interim_objective
    pair_count = ROWS * (SHIFTS + 1) * ROWS_DEV
    grad_images = unnormalize(img_unit, img_len, grad_img.reshape(ROWS, D))
    grad_texts = unnormalize(txt_unit, txt_len, grad_txt.reshape(ROWS, D))
    scaled = accumulated_sums / pair_count
    return (grad_images, grad_texts, scaled[0:1], scaled[1:2], scaled[2:3])
```

```python
import functools

import jax
import jax.numpy as jnp
from jax import lax
from jax.experimental import pallas as pl
from jax.experimental.pallas import tpu as pltpu
from jax.sharding import PartitionSpec as P

MESH = pl.DeviceIdType.MESH
SHIFTS = 4
EPS = 1e-06
RUN = 8
CHUNK = 32
COLS = 384


def ring_stages(b, g, n_blk, n_group):
    x, zl = lax.div(b, RUN), lax.rem(b, RUN)
    y, low = lax.div(g, 4), lax.rem(g, 4)
    zh, core = lax.div(low, 2), lax.rem(low, 2)
    n_x, n_y = n_blk // RUN, n_group // 4
    z = zh * RUN + zl

    def along_z(k):
        other = lax.rem(z + k, 2 * RUN)
        return (x * RUN + lax.rem(other, RUN), y * 4 + lax.div(other, RUN) * 2 + core)

    return [
        (core, [(b, y * 4 + zh * 2 + (1 - core))]),
        (x, [(lax.rem(b + RUN * k, n_blk), g) for k in range(1, n_x)]),
        (y, [(b, lax.rem(g + 4 * k, n_group)) for k in range(1, n_y)]),
        (z, [along_z(k) for k in range(1, 2 * RUN)]),
    ]


def kernel(
    n_blk, n_group, scale_ref, images_ref, texts_ref,
    gimg_ref, gtxt_ref, sums_ref,
    blocks, unit, length, grad, totals, parts,
    send_sem, recv_sem, part_send, part_recv,
):
    rows, width = images_ref.shape
    n_chunks = rows // CHUNK
    b, g = lax.axis_index("blk"), lax.axis_index("group")
    right, left = lax.rem(b + 1, n_blk), lax.rem(b + n_blk - 1, n_blk)
    partner = lax.rem(g + n_group // 2, n_group)
    stages = ring_stages(b, g, n_blk, n_group)

    barrier = pltpu.get_barrier_semaphore()
    peers = [(right, g), (left, g), (b, partner)] + [p for _, line in stages for p in line]
    for peer in peers:
        pl.semaphore_signal(barrier, inc=1, device_id=peer, device_id_type=MESH)

    temperature = jnp.exp(scale_ref[0])
    bias = scale_ref[1]

    for stream, ref in ((0, texts_ref), (1, images_ref)):
        widened = ref[...].astype(jnp.float32)
        size = jnp.sqrt(jnp.sum(widened * widened, axis=-1, keepdims=True) + EPS)
        unit_rows = widened / size
        unit[stream] = unit_rows
        length[stream] = size
        blocks[stream, 0] = unit_rows.astype(jnp.bfloat16)
    totals[...] = jnp.zeros_like(totals)

    def move(stream, hop, chunk):
        last = lax.div(hop, SHIFTS - 1)
        to_blk = last * b + (1 - last) * (stream * left + (1 - stream) * right)
        to_group = last * partner + (1 - last) * g
        at = pl.ds(pl.multiple_of(chunk * CHUNK, CHUNK), CHUNK)
        return pltpu.make_async_remote_copy(
            src_ref=blocks.at[stream, hop, at],
            dst_ref=blocks.at[stream, hop + 1, at],
            send_sem=send_sem.at[stream, hop, chunk],
            recv_sem=recv_sem.at[stream, hop, chunk],
            device_id=(to_blk, to_group),
            device_id_type=MESH,
        )

    def meet(stream, hop, own, add):
        mine, block = blocks[1 - stream, 0], blocks[stream, hop]
        cosine = lax.dot_general(mine, block, (((1,), (1,)), ((), ())), preferred_element_type=jnp.float32)
        logits = temperature * cosine + bias
        if own:
            same = lax.broadcasted_iota(jnp.int32, (rows, rows), 0) == lax.broadcasted_iota(jnp.int32, (rows, rows), 1)
            sign = jnp.where(same, 1.0, -1.0)
            flipped = -sign * logits
        else:
            flipped = logits
        slope = jax.nn.sigmoid(flipped)
        if own:
            slope = -sign * slope
        weights = (temperature * slope).astype(jnp.bfloat16)
        for c in range(0, width, COLS):
            part = jnp.dot(weights, blocks[stream, hop, :, c : c + COLS], preferred_element_type=jnp.float32)
            if add:
                grad[1 - stream, :, c : c + COLS] += part
            else:
                grad[1 - stream, :, c : c + COLS] = part
        counted = 1.0 - jnp.asarray(stream, jnp.float32)
        term = jnp.maximum(flipped, 0.0) + jnp.log1p(jnp.exp(-jnp.abs(flipped)))
        for i, value in enumerate((term, slope * (temperature * cosine), slope)):
            totals[i : i + 1, :] += counted * jnp.sum(value, axis=0, keepdims=True)

    pl.semaphore_wait(barrier, len(peers))

    def first(chunk, carry):
        move(0, 0, chunk).start()
        move(1, 0, chunk).start()
        return carry

    lax.fori_loop(0, n_chunks, first, 0)
    meet(0, 0, True, False)
    meet(1, 0, True, False)

    place = lax.rem(b, RUN)
    high = lax.div(place, RUN // 2)
    edge = (1 - high) * place + high * (RUN - 1 - place)
    near = 1 - high

    def pick(k, table):
        value = jnp.int32(table[-1])
        for i in range(len(table) - 1):
            value = jnp.where(k == i, table[i], value)
        return value

    def visit(k, carry):
        far_0, far_1, far_2 = (pick(k, t) for t in ((0, 0, 0, 1, 1, 1, 0, 1), (0, 1, 0, 0, 1, 1, 0, 1), (0, 1, 0, 1, 0, 1, 0, 1)))
        hop_0, hop_1, hop_2 = (pick(k, t) for t in ((1, 2, 3, 1, 2, 3, 4, 4), (1, 1, 2, 3, 2, 3, 4, 4), (1, 1, 2, 2, 3, 3, 4, 4)))
        far = jnp.where(edge == 0, far_0, jnp.where(edge == 1, far_1, far_2))
        hop = jnp.where(edge == 0, hop_0, jnp.where(edge == 1, hop_1, hop_2))
        stream = far * (1 - near) + (1 - far) * near

        def take(chunk, c):
            move(stream, hop - 1, chunk).wait_recv()

            @pl.when(hop < SHIFTS)
            def _():
                move(stream, hop, chunk).start()

            return c

        lax.fori_loop(0, n_chunks, take, 0)
        meet(stream, hop, False, True)
        return carry

    lax.fori_loop(0, 2 * SHIFTS, visit, 0)

    sums = jnp.sum(totals[...], axis=1, keepdims=True)
    value = jnp.broadcast_to(sums, (8, 128))
    k = 0
    copies = []
    for s, (index, line) in enumerate(stages):
        parts[s, index] = value
        mine = []
        for peer in line:
            copy = pltpu.make_async_remote_copy(
                src_ref=parts.at[s, index],
                dst_ref=parts.at[s, index],
                send_sem=part_send.at[k],
                recv_sem=part_recv.at[k],
                device_id=peer,
                device_id_type=MESH,
            )
            copy.start()
            mine.append(copy)
            k += 1
        if s == 0:
            for stream, out in ((0, gtxt_ref), (1, gimg_ref)):
                gradient, unit_rows = grad[stream], unit[stream]
                along = jnp.sum(unit_rows * gradient, axis=-1, keepdims=True)
                out[...] = (gradient - unit_rows * along) / length[stream]
        for copy in mine:
            copy.wait_recv()
        value = parts[s, 0]
        for i in range(1, len(line) + 1):
            value = value + parts[s, i]
        copies += mine
    count = n_blk * n_group * rows * (SHIFTS + 1) * rows
    sums_ref[...] = value / count

    def sent(chunk, carry):
        for stream in (0, 1):
            for hop in range(SHIFTS):
                move(stream, hop, chunk).wait_send()
        return carry

    lax.fori_loop(0, n_chunks, sent, 0)
    for copy in copies:
        copy.wait_send()


def solution(mesh):
    n_blk, n_group = mesh.shape["blk"], mesh.shape["group"]

    def body(images, texts, exponent_of_multiplier, bias):
        rows, width = images.shape
        n_chunks = rows // CHUNK
        n_parts = 1 + (n_blk // RUN - 1) + (n_group // 4 - 1) + (2 * RUN - 1)
        scale = jnp.concatenate([exponent_of_multiplier, bias])
        vmem = pl.BlockSpec(memory_space=pltpu.VMEM)
        grad_images, grad_texts, sums = pl.pallas_call(
            functools.partial(kernel, n_blk, n_group),
            out_shape=[
                jax.ShapeDtypeStruct((rows, width), jnp.float32),
                jax.ShapeDtypeStruct((rows, width), jnp.float32),
                jax.ShapeDtypeStruct((8, 128), jnp.float32),
            ],
            in_specs=[pl.BlockSpec(memory_space=pltpu.SMEM), vmem, vmem],
            out_specs=[vmem, vmem, vmem],
            scratch_shapes=[
                pltpu.VMEM((2, SHIFTS + 1, rows, width), jnp.bfloat16),
                pltpu.VMEM((2, rows, width), jnp.float32),
                pltpu.VMEM((2, rows, 1), jnp.float32),
                pltpu.VMEM((2, rows, width), jnp.float32),
                pltpu.VMEM((8, rows), jnp.float32),
                pltpu.VMEM((4, 2 * RUN, 8, 128), jnp.float32),
                pltpu.SemaphoreType.DMA((2, SHIFTS, n_chunks)),
                pltpu.SemaphoreType.DMA((2, SHIFTS, n_chunks)),
                pltpu.SemaphoreType.DMA((n_parts,)),
                pltpu.SemaphoreType.DMA((n_parts,)),
            ],
            compiler_params=pltpu.CompilerParams(
                collective_id=0, has_side_effects=True, vmem_limit_bytes=48 * 2**20
            ),
        )(scale, images, texts)
        return grad_images, grad_texts, sums[0, 0:1], sums[1, 0:1], sums[2, 0:1]

    in_specs = (P(("blk", "group"), None), P(("blk", "group"), None), P(), P())
    out_specs = (P(("blk", "group"), None), P(("blk", "group"), None), P(), P(), P())
    return jax.shard_map(body, mesh=mesh, in_specs=in_specs, out_specs=out_specs, check_vma=False)
```

```python
import functools

import jax
import jax.numpy as jnp
from jax import lax
from jax.experimental import pallas as pl
from jax.experimental.pallas import tpu as pltpu
from jax.sharding import PartitionSpec as P

MESH = pl.DeviceIdType.MESH
SHIFTS = 4
EPS = 1e-06
RUN = 8
CHUNK = 32
WRAP = 0
SWAP = 0
REDUCE = (0, 0, 1, 2)
COLS = 384


def ring_stages(b, g, n_blk, n_group):
    x, zl = lax.div(b, RUN), lax.rem(b, RUN)
    y, low = lax.div(g, 4), lax.rem(g, 4)
    zh, core = lax.div(low, 2), lax.rem(low, 2)
    n_x, n_y = n_blk // RUN, n_group // 4
    z = zh * RUN + zl

    def along_z(k):
        other = lax.rem(z + k, 2 * RUN)
        return (x * RUN + lax.rem(other, RUN), y * 4 + lax.div(other, RUN) * 2 + core)

    return [
        (core, [(b, y * 4 + zh * 2 + (1 - core))]),
        (x, [(lax.rem(b + RUN * k, n_blk), g) for k in range(1, n_x)]),
        (y, [(b, lax.rem(g + 4 * k, n_group)) for k in range(1, n_y)]),
        (z, [along_z(k) for k in range(1, 2 * RUN)]),
    ]


def kernel(
    n_blk, n_group, images_hbm, texts_hbm, exponent_hbm, bias_hbm,
    gimg_ref, gtxt_ref, sums_ref,
    raw, exponent_ref, bias_ref, blocks, unit, length, grad, totals, parts,
    in_sem, send_sem, recv_sem, part_send, part_recv, ready, know_x, know_y, know_z,
):
    rows, width = images_hbm.shape
    n_chunks = rows // CHUNK
    b, g = lax.axis_index("blk"), lax.axis_index("group")
    right, left = lax.rem(b + 1, n_blk), lax.rem(b + n_blk - 1, n_blk)
    partner = lax.rem(g + n_group // 2, n_group)
    stages = ring_stages(b, g, n_blk, n_group)

    loads = [
        pltpu.make_async_copy(src, dst, in_sem.at[k])
        for k, (src, dst) in enumerate(
            ((texts_hbm, raw.at[0]), (images_hbm, raw.at[1]), (exponent_hbm, exponent_ref), (bias_hbm, bias_ref))
        )
    ]
    for load in loads:
        load.start()

    x, place = lax.div(b, RUN), lax.rem(b, RUN)
    low = lax.rem(g, 4)
    z_hi, core = lax.div(low, 2), lax.rem(low, 2)
    z, n_z = z_hi * RUN + place, 2 * RUN

    def at_x(k):
        return (lax.rem(b + k * RUN + n_blk, n_blk), g)

    def at_y(k):
        return (b, lax.rem(g + 4 * k + n_group, n_group))

    def at_z(k):
        return (x * RUN + lax.rem(z + k, RUN), g + 2 * (lax.div(z + k, RUN) - z_hi))

    def tell(semaphore, device):
        pl.semaphore_signal(semaphore, inc=1, device_id=device, device_id_type=MESH)

    def tell_z(semaphore, k):
        @pl.when(z >= k)
        def _():
            tell(semaphore, at_z(-k))

        @pl.when(z + k < n_z)
        def _():
            tell(semaphore, at_z(k))

    def heard_z(k):
        return jnp.where(z >= k, 1, 0) + jnp.where(z + k < n_z, 1, 0)

    barrier = pltpu.get_barrier_semaphore()
    for device in ((b, g + 1 - 2 * core), at_x(1), at_x(-1), at_y(1), at_y(-1)):
        tell(barrier, device)
    tell_z(barrier, 1)

    @pl.when(place == 0)
    def _():
        tell(barrier, (left, g))

    def prepare(stream):
        loads[stream].wait()
        widened = raw[stream].astype(jnp.float32)
        size = jnp.sqrt(jnp.sum(widened * widened, axis=-1, keepdims=True) + EPS)
        unit_rows = widened / size
        unit[stream] = unit_rows
        length[stream] = size
        blocks[stream, 0] = unit_rows.astype(jnp.bfloat16)

    prepare(0)
    totals[...] = jnp.zeros_like(totals)
    loads[2].wait()
    loads[3].wait()
    temperature = jnp.exp(jnp.broadcast_to(exponent_ref[0], (1, 1)))
    bias = bias_ref[0]

    def move(stream, hop, chunk):
        if hop == SHIFTS - 1:
            target = (b, partner)
        else:
            target = (right, g) if stream == 0 else (left, g)
        at = pl.ds(pl.multiple_of(chunk * CHUNK, CHUNK), CHUNK)
        return pltpu.make_async_remote_copy(
            src_ref=blocks.at[stream, hop, at],
            dst_ref=blocks.at[stream, hop + 1, at],
            send_sem=send_sem.at[stream, hop, chunk],
            recv_sem=recv_sem.at[stream, hop, chunk],
            device_id=target,
            device_id_type=MESH,
        )

    def meet(stream, hop, own, add):
        mine, block = blocks[1 - stream, 0], blocks[stream, hop]
        cosine = lax.dot_general(mine, block, (((1,), (1,)), ((), ())), preferred_element_type=jnp.float32)
        logits = temperature * cosine + bias
        if own:
            same = lax.broadcasted_iota(jnp.int32, (rows, rows), 0) == lax.broadcasted_iota(jnp.int32, (rows, rows), 1)
            sign = jnp.where(same, 1.0, -1.0)
            flipped = -sign * logits
        else:
            flipped = logits
        slope = jax.nn.sigmoid(flipped)
        if own:
            slope = -sign * slope
        weights = (temperature * slope).astype(jnp.bfloat16)
        for c in range(0, width, COLS):
            part = jnp.dot(weights, blocks[stream, hop, :, c : c + COLS], preferred_element_type=jnp.float32)
            if add:
                grad[1 - stream, :, c : c + COLS] += part
            else:
                grad[1 - stream, :, c : c + COLS] = part
        if stream == 1:
            return
        term = jnp.maximum(flipped, 0.0) + jnp.log1p(jnp.exp(-jnp.abs(flipped)))
        for i, value in enumerate((term, slope * (temperature * cosine), slope)):
            totals[i : i + 1, :] += jnp.sum(value, axis=0, keepdims=True)

    pl.semaphore_wait(barrier, 5 + heard_z(1) + jnp.where(place == RUN - 1, 1, 0))
    tell(ready, (right, g))
    for k in (1, -1):
        tell(know_x, at_x(k))
        tell(know_y.at[0], at_y(k))
    tell_z(know_z.at[0], 1)

    def lag(stream, hop):
        before = place if stream == 0 else RUN - 1 - place
        ring = min(hop, SHIFTS - 1)
        late = jnp.where(before < ring, 1, 0)
        return hop + late * WRAP + (SWAP if hop == SHIFTS else 0), late

    def reduce_stage(s):
        index, line = stages[s]
        if s == len(stages) - 1:
            pl.semaphore_wait(know_z.at[3], heard_z(8))
        if s == 0:
            value = jnp.broadcast_to(jnp.sum(totals[...], axis=1, keepdims=True), (8, 128))
        else:
            value = collect(s - 1)
        parts[s, index] = value
        for copy in part_copies(s):
            copy.start()

    def part_copies(s):
        index, line = stages[s]
        first = sum(len(stages[i][1]) for i in range(s))
        return [
            pltpu.make_async_remote_copy(
                src_ref=parts.at[s, index],
                dst_ref=parts.at[s, index],
                send_sem=part_send.at[first + k],
                recv_sem=part_recv.at[first + k],
                device_id=peer,
                device_id_type=MESH,
            )
            for k, peer in enumerate(line)
        ]

    def collect(s):
        for copy in part_copies(s):
            copy.wait_recv()
        value = parts[s, 0]
        for i in range(1, len(stages[s][1]) + 1):
            value = value + parts[s, i]
        return value

    def finish(stream, out):
        gradient, unit_rows = grad[stream], unit[stream]
        along = jnp.sum(unit_rows * gradient, axis=-1, keepdims=True)
        out[...] = (gradient - unit_rows * along) / length[stream]

    def round_of(r, carry):
        for stream in (0, 1):
            chunk = r - stream * n_chunks

            @pl.when((chunk >= 0) & (chunk < n_chunks))
            def _():
                move(stream, 0, chunk).start()

        @pl.when(r == 1)
        def _():
            pl.semaphore_wait(know_x, 2)
            pl.semaphore_wait(know_y.at[0], 2)
            pl.semaphore_wait(know_z.at[0], heard_z(1))
            for k in (2, -2):
                tell(know_y.at[1], at_y(k))
            tell_z(know_z.at[1], 2)

        @pl.when(r == 2)
        def _():
            pl.semaphore_wait(know_y.at[1], 2)
            pl.semaphore_wait(know_z.at[1], heard_z(2))
            tell_z(know_z.at[2], 4)

        @pl.when(r == 3)
        def _():
            pl.semaphore_wait(know_z.at[2], heard_z(4))
            tell_z(know_z.at[3], 8)

        @pl.when(r == n_chunks - 1)
        def _():
            pl.semaphore_wait(ready, 1)

        for want in (0, 1):
            for stream in (0, 1):
                for hop in range(1, SHIFTS):
                    rounds, late = lag(stream, hop)
                    chunk = r - stream * n_chunks - rounds

                    @pl.when((chunk >= 0) & (chunk < n_chunks) & (late == want))
                    def _():
                        move(stream, hop - 1, chunk).wait_recv()
                        move(stream, hop, chunk).start()

        @pl.when(r == 0)
        def _():
            prepare(1)
            meet(0, 0, True, False)
            meet(1, 0, True, False)

        for stream in (0, 1):
            for hop in range(1, SHIFTS + 1):
                rounds, _ = lag(stream, hop)

                @pl.when(r == (stream + 1) * n_chunks - 1 + rounds)
                def _():
                    if hop == SHIFTS:
                        def arrived(chunk, c):
                            move(stream, hop - 1, chunk).wait_recv()
                            return c

                        lax.fori_loop(0, n_chunks, arrived, 0)
                    meet(stream, hop, False, True)

        for s in range(len(stages)):

            @pl.when(r == reduce_at + REDUCE[s])
            def _():
                reduce_stage(s)

        @pl.when(r == reduce_at + 1)
        def _():
            finish(1, gimg_ref)

        return carry

    reduce_at = n_chunks - 1 + SHIFTS + WRAP + SWAP
    n_rounds = 2 * n_chunks + SHIFTS + WRAP + SWAP
    assert reduce_at + REDUCE[-1] < n_rounds
    lax.fori_loop(0, n_rounds, round_of, 0)

    finish(0, gtxt_ref)
    count = n_blk * n_group * rows * (SHIFTS + 1) * rows
    sums_ref[...] = collect(len(stages) - 1) / count

    def sent(chunk, carry):
        for stream in (0, 1):
            for hop in range(SHIFTS):
                move(stream, hop, chunk).wait_send()
        return carry

    lax.fori_loop(0, n_chunks, sent, 0)
    for s in range(len(stages)):
        for copy in part_copies(s):
            copy.wait_send()


def solution(mesh):
    n_blk, n_group = mesh.shape["blk"], mesh.shape["group"]

    def body(images, texts, exponent_of_multiplier, bias):
        rows, width = images.shape
        n_chunks = rows // CHUNK
        n_parts = 1 + (n_blk // RUN - 1) + (n_group // 4 - 1) + (2 * RUN - 1)
        vmem = pl.BlockSpec(memory_space=pltpu.VMEM)
        grad_images, grad_texts, sums = pl.pallas_call(
            functools.partial(kernel, n_blk, n_group),
            out_shape=[
                jax.ShapeDtypeStruct((rows, width), jnp.float32),
                jax.ShapeDtypeStruct((rows, width), jnp.float32),
                jax.ShapeDtypeStruct((8, 128), jnp.float32),
            ],
            in_specs=[pl.BlockSpec(memory_space=pl.ANY)] * 4,
            out_specs=[vmem, vmem, vmem],
            scratch_shapes=[
                pltpu.VMEM((2, rows, width), jnp.bfloat16),
                pltpu.SMEM((1,), jnp.float32),
                pltpu.SMEM((1,), jnp.float32),
                pltpu.VMEM((2, SHIFTS + 1, rows, width), jnp.bfloat16),
                pltpu.VMEM((2, rows, width), jnp.float32),
                pltpu.VMEM((2, rows, 1), jnp.float32),
                pltpu.VMEM((2, rows, width), jnp.float32),
                pltpu.VMEM((8, rows), jnp.float32),
                pltpu.VMEM((4, 2 * RUN, 8, 128), jnp.float32),
                pltpu.SemaphoreType.DMA((4,)),
                pltpu.SemaphoreType.DMA((2, SHIFTS, n_chunks)),
                pltpu.SemaphoreType.DMA((2, SHIFTS, n_chunks)),
                pltpu.SemaphoreType.DMA((n_parts,)),
                pltpu.SemaphoreType.DMA((n_parts,)),
                pltpu.SemaphoreType.REGULAR,
                pltpu.SemaphoreType.REGULAR,
                pltpu.SemaphoreType.REGULAR((2,)),
                pltpu.SemaphoreType.REGULAR((4,)),
            ],
            compiler_params=pltpu.CompilerParams(
                collective_id=0, has_side_effects=True, vmem_limit_bytes=48 * 2**20
            ),
        )(images, texts, exponent_of_multiplier, bias)
        return grad_images, grad_texts, sums[0, 0:1], sums[1, 0:1], sums[2, 0:1]

    in_specs = (P(("blk", "group"), None), P(("blk", "group"), None), P(), P())
    out_specs = (P(("blk", "group"), None), P(("blk", "group"), None), P(), P(), P())
    return jax.shard_map(body, mesh=mesh, in_specs=in_specs, out_specs=out_specs, check_vma=False)
```

```python
import functools

import jax
import jax.numpy as jnp
from jax import lax
from jax.experimental import pallas as pl
from jax.experimental.pallas import tpu as pltpu
from jax.sharding import PartitionSpec as P

MESH = pl.DeviceIdType.MESH
SHIFTS = 4
EPS = 1e-06
RUN = 8
CHUNK = 32
WRAP = 0
SWAP = 0
REDUCE = (0, 1, 2)
COLS = 384


def ring_stages(b, g, n_blk, n_group):
    x, zl = lax.div(b, RUN), lax.rem(b, RUN)
    y, low = lax.div(g, 4), lax.rem(g, 4)
    zh, core = lax.div(low, 2), lax.rem(low, 2)
    n_x, n_y = n_blk // RUN, n_group // 4
    z = zh * RUN + zl

    def along_z(k):
        other = lax.rem(z + k, 2 * RUN)
        return (x * RUN + lax.rem(other, RUN), y * 4 + lax.div(other, RUN) * 2 + core)

    return [
        (
            x * 2 + core,
            [
                (lax.rem(b + RUN * k, n_blk), g + flip * (1 - 2 * core))
                for flip in (0, 1)
                for k in range(n_x)
                if (flip, k) != (0, 0)
            ],
        ),
        (y, [(b, lax.rem(g + 4 * k, n_group)) for k in range(1, n_y)]),
        (z, [along_z(k) for k in range(1, 2 * RUN)]),
    ]


def kernel(
    n_blk, n_group, images_ref, texts_ref, exponent_ref, bias_ref,
    gimg_ref, gtxt_ref, sums_ref,
    blocks, unit, length, grad, totals, parts,
    send_sem, recv_sem, part_send, part_recv, ready, know_core, know_x, know_y, know_z,
):
    rows, width = images_ref.shape
    n_chunks = rows // CHUNK
    b, g = lax.axis_index("blk"), lax.axis_index("group")
    right, left = lax.rem(b + 1, n_blk), lax.rem(b + n_blk - 1, n_blk)
    partner = lax.rem(g + n_group // 2, n_group)
    stages = ring_stages(b, g, n_blk, n_group)

    x, place = lax.div(b, RUN), lax.rem(b, RUN)
    low = lax.rem(g, 4)
    z_hi, core = lax.div(low, 2), lax.rem(low, 2)
    z, n_z = z_hi * RUN + place, 2 * RUN

    def at_x(k):
        return (lax.rem(b + k * RUN + n_blk, n_blk), g)

    def at_y(k):
        return (b, lax.rem(g + 4 * k + n_group, n_group))

    def at_z(k):
        return (x * RUN + lax.rem(z + k, RUN), g + 2 * (lax.div(z + k, RUN) - z_hi))

    def tell(semaphore, device):
        pl.semaphore_signal(semaphore, inc=1, device_id=device, device_id_type=MESH)

    def tell_z(semaphore, k):
        @pl.when(z >= k)
        def _():
            tell(semaphore, at_z(-k))

        @pl.when(z + k < n_z)
        def _():
            tell(semaphore, at_z(k))

    def heard_z(k):
        return jnp.where(z >= k, 1, 0) + jnp.where(z + k < n_z, 1, 0)

    barrier = pltpu.get_barrier_semaphore()
    for device in ((b, g + 1 - 2 * core), at_x(1), at_x(-1), at_y(1), at_y(-1)):
        tell(barrier, device)
    tell_z(barrier, 1)

    @pl.when(place == 0)
    def _():
        tell(barrier, (left, g))

    def prepare(stream):
        widened = (texts_ref, images_ref)[stream][...].astype(jnp.float32)
        size = jnp.sqrt(jnp.sum(widened * widened, axis=-1, keepdims=True) + EPS)
        unit_rows = widened / size
        unit[stream] = unit_rows
        length[stream] = size
        blocks[stream, 0] = unit_rows.astype(jnp.bfloat16)

    prepare(0)
    totals[...] = jnp.zeros_like(totals)
    temperature = jnp.exp(jnp.broadcast_to(exponent_ref[0], (1, 1)))
    bias = bias_ref[0]

    def move(stream, hop, chunk):
        if hop == SHIFTS - 1:
            target = (b, partner)
        else:
            target = (right, g) if stream == 0 else (left, g)
        at = pl.ds(pl.multiple_of(chunk * CHUNK, CHUNK), CHUNK)
        return pltpu.make_async_remote_copy(
            src_ref=blocks.at[stream, hop, at],
            dst_ref=blocks.at[stream, hop + 1, at],
            send_sem=send_sem.at[stream, hop, chunk],
            recv_sem=recv_sem.at[stream, hop, chunk],
            device_id=target,
            device_id_type=MESH,
        )

    def meet(stream, hop, own, add):
        mine, block = blocks[1 - stream, 0], blocks[stream, hop]
        cosine = lax.dot_general(mine, block, (((1,), (1,)), ((), ())), preferred_element_type=jnp.float32)
        logits = temperature * cosine + bias
        if own:
            same = lax.broadcasted_iota(jnp.int32, (rows, rows), 0) == lax.broadcasted_iota(jnp.int32, (rows, rows), 1)
            sign = jnp.where(same, 1.0, -1.0)
            flipped = -sign * logits
        else:
            flipped = logits
        slope = jax.nn.sigmoid(flipped)
        if own:
            slope = -sign * slope
        weights = (temperature * slope).astype(jnp.bfloat16)
        for c in range(0, width, COLS):
            part = jnp.dot(weights, blocks[stream, hop, :, c : c + COLS], preferred_element_type=jnp.float32)
            if add:
                grad[1 - stream, :, c : c + COLS] += part
            else:
                grad[1 - stream, :, c : c + COLS] = part
        if stream == 1:
            return
        term = jnp.maximum(flipped, 0.0) + jnp.log1p(jnp.exp(-jnp.abs(flipped)))
        for i, value in enumerate((term, slope * (temperature * cosine), slope)):
            totals[i : i + 1, :] += jnp.sum(value, axis=0, keepdims=True)

    pl.semaphore_wait(barrier, 5 + heard_z(1) + jnp.where(place == RUN - 1, 1, 0))
    tell(ready, (right, g))
    for k in (1, -1):
        tell(know_x, at_x(k))
        tell(know_y.at[0], at_y(k))
    tell_z(know_z.at[0], 1)

    def lag(stream, hop):
        before = place if stream == 0 else RUN - 1 - place
        ring = min(hop, SHIFTS - 1)
        late = jnp.where(before < ring, 1, 0)
        return hop + late * WRAP + (SWAP if hop == SHIFTS else 0), late

    def reduce_stage(s):
        index, line = stages[s]
        if s == len(stages) - 1:
            pl.semaphore_wait(know_z.at[3], heard_z(8))
        if s == 0:
            value = jnp.broadcast_to(jnp.sum(totals[...], axis=1, keepdims=True), (8, 128))
        else:
            value = collect(s - 1)
        parts[s, index] = value
        for copy in part_copies(s):
            copy.start()

    def part_copies(s):
        index, line = stages[s]
        first = sum(len(stages[i][1]) for i in range(s))
        return [
            pltpu.make_async_remote_copy(
                src_ref=parts.at[s, index],
                dst_ref=parts.at[s, index],
                send_sem=part_send.at[first + k],
                recv_sem=part_recv.at[first + k],
                device_id=peer,
                device_id_type=MESH,
            )
            for k, peer in enumerate(line)
        ]

    def collect(s):
        for copy in part_copies(s):
            copy.wait_recv()
        value = parts[s, 0]
        for i in range(1, len(stages[s][1]) + 1):
            value = value + parts[s, i]
        return value

    def finish(stream, out):
        gradient, unit_rows = grad[stream], unit[stream]
        along = jnp.sum(unit_rows * gradient, axis=-1, keepdims=True)
        out[...] = (gradient - unit_rows * along) / length[stream]

    def round_of(r, carry):
        for stream in (0, 1):
            chunk = r - stream * n_chunks

            @pl.when((chunk >= 0) & (chunk < n_chunks))
            def _():
                move(stream, 0, chunk).start()

        @pl.when(r == 1)
        def _():
            pl.semaphore_wait(know_x, 2)
            tell(know_core, (b, g + 1 - 2 * core))
            pl.semaphore_wait(know_y.at[0], 2)
            pl.semaphore_wait(know_z.at[0], heard_z(1))
            for k in (2, -2):
                tell(know_y.at[1], at_y(k))
            tell_z(know_z.at[1], 2)

        @pl.when(r == 2)
        def _():
            pl.semaphore_wait(know_core, 1)
            pl.semaphore_wait(know_y.at[1], 2)
            pl.semaphore_wait(know_z.at[1], heard_z(2))
            tell_z(know_z.at[2], 4)

        @pl.when(r == 3)
        def _():
            pl.semaphore_wait(know_z.at[2], heard_z(4))
            tell_z(know_z.at[3], 8)

        @pl.when(r == n_chunks - 1)
        def _():
            pl.semaphore_wait(ready, 1)

        for want in (0, 1):
            for stream in (0, 1):
                for hop in range(1, SHIFTS):
                    rounds, late = lag(stream, hop)
                    chunk = r - stream * n_chunks - rounds

                    @pl.when((chunk >= 0) & (chunk < n_chunks) & (late == want))
                    def _():
                        move(stream, hop - 1, chunk).wait_recv()
                        move(stream, hop, chunk).start()

        @pl.when(r == 0)
        def _():
            prepare(1)
            meet(0, 0, True, False)
            meet(1, 0, True, False)

        for stream in (0, 1):
            for hop in range(1, SHIFTS + 1):
                rounds, _ = lag(stream, hop)

                @pl.when(r == (stream + 1) * n_chunks - 1 + rounds)
                def _():
                    if hop == SHIFTS:
                        def arrived(chunk, c):
                            move(stream, hop - 1, chunk).wait_recv()
                            return c

                        lax.fori_loop(0, n_chunks, arrived, 0)
                    meet(stream, hop, False, True)

        for s in range(len(stages)):

            @pl.when(r == reduce_at + REDUCE[s])
            def _():
                reduce_stage(s)

        @pl.when(r == reduce_at + 1)
        def _():
            finish(1, gimg_ref)

        return carry

    reduce_at = n_chunks - 1 + SHIFTS + WRAP + SWAP
    n_rounds = 2 * n_chunks + SHIFTS + WRAP + SWAP
    assert reduce_at + REDUCE[-1] < n_rounds
    lax.fori_loop(0, n_rounds, round_of, 0)

    finish(0, gtxt_ref)
    count = n_blk * n_group * rows * (SHIFTS + 1) * rows
    sums_ref[...] = collect(len(stages) - 1) / count

    def sent(chunk, carry):
        for stream in (0, 1):
            for hop in range(SHIFTS):
                move(stream, hop, chunk).wait_send()
        return carry

    lax.fori_loop(0, n_chunks, sent, 0)
    for s in range(len(stages)):
        for copy in part_copies(s):
            copy.wait_send()


def solution(mesh):
    n_blk, n_group = mesh.shape["blk"], mesh.shape["group"]

    def body(images, texts, exponent_of_multiplier, bias):
        rows, width = images.shape
        n_chunks = rows // CHUNK
        n_parts = (2 * (n_blk // RUN) - 1) + (n_group // 4 - 1) + (2 * RUN - 1)
        vmem = pl.BlockSpec(memory_space=pltpu.VMEM)
        grad_images, grad_texts, sums = pl.pallas_call(
            functools.partial(kernel, n_blk, n_group),
            out_shape=[
                jax.ShapeDtypeStruct((rows, width), jnp.float32),
                jax.ShapeDtypeStruct((rows, width), jnp.float32),
                jax.ShapeDtypeStruct((8, 128), jnp.float32),
            ],
            in_specs=[vmem, vmem, pl.BlockSpec(memory_space=pltpu.SMEM), pl.BlockSpec(memory_space=pltpu.SMEM)],
            out_specs=[vmem, vmem, vmem],
            scratch_shapes=[
                pltpu.VMEM((2, SHIFTS + 1, rows, width), jnp.bfloat16),
                pltpu.VMEM((2, rows, width), jnp.float32),
                pltpu.VMEM((2, rows, 1), jnp.float32),
                pltpu.VMEM((2, rows, width), jnp.float32),
                pltpu.VMEM((8, rows), jnp.float32),
                pltpu.VMEM((3, 2 * RUN, 8, 128), jnp.float32),
                pltpu.SemaphoreType.DMA((2, SHIFTS, n_chunks)),
                pltpu.SemaphoreType.DMA((2, SHIFTS, n_chunks)),
                pltpu.SemaphoreType.DMA((n_parts,)),
                pltpu.SemaphoreType.DMA((n_parts,)),
                pltpu.SemaphoreType.REGULAR,
                pltpu.SemaphoreType.REGULAR,
                pltpu.SemaphoreType.REGULAR,
                pltpu.SemaphoreType.REGULAR((2,)),
                pltpu.SemaphoreType.REGULAR((4,)),
            ],
            compiler_params=pltpu.CompilerParams(
                collective_id=0, has_side_effects=True, vmem_limit_bytes=48 * 2**20
            ),
        )(images, texts, exponent_of_multiplier, bias)
        return grad_images, grad_texts, sums[0, 0:1], sums[1, 0:1], sums[2, 0:1]

    in_specs = (P(("blk", "group"), None), P(("blk", "group"), None), P(), P())
    out_specs = (P(("blk", "group"), None), P(("blk", "group"), None), P(), P(), P())
    return jax.shard_map(body, mesh=mesh, in_specs=in_specs, out_specs=out_specs, check_vma=False)
```
